32 devices in a mesh: parts: 2 (over y), expert: 4 (over x, core), seq: 4 (over z).
Axes of the slice: x: 2, y: 2, z: 4, core: 2. Of those that a mesh axis runs over, the one named last changes fastest.
Arguments:
- tokens: bfloat16 [1024, 5120], P(('parts', 'expert'), 'seq'), parts along dimension 0, may hold values from -6 to 6
- expert_ids: int32 [1024, 6], P(('parts', 'expert')), parts along dimension 0, may hold values from 0 to 7, as said below
- gates: float32 [1024, 6], P(('parts', 'expert')), parts along dimension 0, may hold values from 0.1 to 2
- hot_list: int32 [4], P('parts'), parts along dimension 0, may hold values from 0 to 7, as said below
- w_gate: bfloat16 [8, 5120, 1536], P('expert', None, 'seq'), may hold values from -0.078125 to 0.078125
- w_up: bfloat16 [8, 5120, 1536], P('expert', None, 'seq'), may hold values from -0.078125 to 0.078125
- w_down: bfloat16 [8, 1536, 5120], P('expert', 'seq'), may hold values from -0.15625 to 0.15625
Outputs:
- moved: bfloat16 [1024, 5120], P(('parts', 'expert'), 'seq'), parts along dimension 0
The draws below stay inside these ranges and needn't reach their ends.
There are 2 independent parts, one for each index of `parts`. The reference program is written for one: setup_inputs(seed, part) draws one part's arguments, and reference() takes and returns one part's arrays. A program takes and returns all parts, laid end to end along the dimension named above; an argument that names none is the same for every part. Nothing has to cross between parts.
Inputs may be any that keep to these rules, and one draw needn't show every extreme that they name: `expert_ids`: each row names 6 different experts. `hot_list`: 2 different experts.
All inputs are finite; a program needn't handle non-finite values.
Results may differ from the reference program's by a relative error of at most 0.0058.
Values may be sent and summed in bfloat16 or wider, within the bound.
No kernel may reach another device: no remote copies, remote signals or barrier semaphores. Data moves between devices by JAX's collectives and lax.ppermute only.
A program may use at most 192 MiB of HBM per device.

```python
import math
import jax
import jax.numpy as jnp
from jax import lax

D = 5120
FF = 1536
TOP = 6
HOT = 2
TOK_DEV = 128
EXPERTS = 8
TOKENS = 512
CAP = 72
N_EXPERT = 4
N_SEQ = 4


def hot_experts(key):
    return jax.random.permutation(key, EXPERTS)[:HOT].astype(jnp.int32)


def draw_hot_list(key, part):
    return hot_experts(key)


def draw_expert_ids(key, part):
    chosen = hot_experts(key)
    key = jax.random.fold_in(key, 7)
    first, second = jax.random.split(key)
    noise = jax.random.randint(first, (TOKENS, EXPERTS), 0, 1000)
    favour = jax.random.randint(second, (EXPERTS,), 0, 400)
    numbers = jnp.arange(EXPERTS, dtype=jnp.int32)
    boost = jnp.where(jnp.any(numbers[:, None] == chosen[None, :], axis=1), 600, 0)
    score = (noise + favour[None, :] + boost[None, :]) * EXPERTS + numbers[None, :]
    return lax.top_k(score, TOP)[1].astype(jnp.int32)


def steps_of(key, shape, shards, low, top_value):
    level = 1.0
    for axis_at, shards_of in shards:
        steps = jax.random.uniform(jax.random.fold_in(jax.random.fold_in(key, 6), axis_at), (shards_of,), jnp.float32, low / len(shards), top_value / len(shards))
        level = level * jnp.repeat(jnp.exp(steps), shape[axis_at] // shards_of).reshape((-1,) + (1,) * (len(shape) - 1 - axis_at))
    return level


def gaussian(key, shape, spread, reach, cuts=(), kind=jnp.bfloat16):
    factor_of = steps_of(key, shape, cuts, -0.22, 0.18) if cuts else 1.0
    values = jax.random.normal(key, shape, jnp.float32) * spread * factor_of
    return jnp.minimum(jnp.maximum(values, -reach), reach).astype(kind)


def setup_inputs(seed: int = 0, part: int = 0) -> dict:
    key_list = jax.random.split(jax.random.key(seed), 8)
    own_keys = jax.random.split(jax.random.fold_in(key_list[7], part), 8)
    tokens = gaussian(own_keys[0], (TOKENS, D), 1.0, 6.0, ((0, 4), (1, 4)))
    expert_ids = draw_expert_ids(jax.random.fold_in(jax.random.fold_in(key_list[7], part), 71), part)
    gates = jnp.clip(jnp.exp(math.log(2.0) - 2.9957323 * jax.random.uniform(own_keys[2], (TOKENS, TOP), jnp.float32) ** steps_of(own_keys[2], (TOKENS, TOP), ((0, 4),), -0.2, 0.2)), 0.1, 2.0)
    hot_list = draw_hot_list(jax.random.fold_in(jax.random.fold_in(key_list[7], part), 71), part)
    w_gate = gaussian(key_list[4], (EXPERTS, D, FF), D ** -0.5, 0.078125, ((0, 4), (2, 4)))
    w_up = gaussian(key_list[5], (EXPERTS, D, FF), D ** -0.5, 0.078125, ((0, 4), (2, 4)))
    w_down = gaussian(key_list[6], (EXPERTS, FF, D), FF ** -0.5, 0.15625, ((0, 4), (1, 4)))
    return {"tokens": tokens, "expert_ids": expert_ids, "gates": gates, "hot_list": hot_list, "w_gate": w_gate, "w_up": w_up, "w_down": w_down}


def expert_apply(rows, gate_part, up_part, down_part):
    gate_value = jnp.dot(rows, gate_part, preferred_element_type=jnp.float32)
    up_value = jnp.dot(rows, up_part, preferred_element_type=jnp.float32)
    hidden = (jax.nn.silu(gate_value) * up_value).astype(jnp.bfloat16)
    slice_width = FF // N_SEQ
    result = jnp.zeros((rows.shape[0], D), jnp.float32)
    for column in range(N_SEQ):
        piece_sum = jnp.dot(hidden[:, column * slice_width:(column + 1) * slice_width],
                            down_part[column * slice_width:(column + 1) * slice_width],
                            preferred_element_type=jnp.float32)
        rounded = lax.optimization_barrier(piece_sum.astype(jnp.bfloat16))
        result = result + rounded.astype(jnp.float32)
    return result


def reference(tokens, expert_ids, gates, hot_list, w_gate, w_up, w_down):
    route_total = TOKENS * TOP
    flat_ids = expert_ids.reshape(-1).astype(jnp.int32)
    flat_rows = (jnp.arange(route_total, dtype=jnp.int32) // TOP).astype(jnp.int32)
    onehot = (flat_ids[:, None] == jnp.arange(EXPERTS, dtype=jnp.int32)[None, :]).astype(jnp.int32)
    grouped = onehot.reshape(N_EXPERT, TOK_DEV * TOP, EXPERTS)
    earlier = (jnp.cumsum(grouped, axis=1) - grouped).reshape(route_total, EXPERTS)
    slot_index = jnp.sum(earlier * onehot, axis=1).astype(jnp.int32)
    source = (flat_rows // TOK_DEV).astype(jnp.int32)
    hot_route = jnp.any(flat_ids[:, None] == hot_list[None, :], axis=1)
    kept_cold = jnp.logical_and(jnp.logical_not(hot_route), slot_index < CAP)
    buffer_size = EXPERTS * N_EXPERT * CAP
    buffer_place = jnp.where(kept_cold, (flat_ids * N_EXPERT + source) * CAP + slot_index, buffer_size).astype(jnp.int32)
    slot_rows = jnp.zeros((buffer_size,), jnp.int32).at[buffer_place].set(flat_rows, mode="drop")
    gathered = tokens[slot_rows].reshape(EXPERTS, N_EXPERT * CAP, D)

    def one_expert(operands):
        return expert_apply(operands[0], operands[1], operands[2], operands[3])

    cold = lax.map(one_expert, (gathered, w_gate, w_up, w_down)).reshape(buffer_size, D)
    route_place = jnp.minimum(buffer_place, buffer_size - 1).reshape(TOKENS, TOP)
    route_weight = jnp.where(kept_cold, gates.reshape(-1), 0.0).reshape(TOKENS, TOP)
    combined = jnp.zeros((TOKENS, D), jnp.float32)
    for route_index in range(TOP):
        combined = combined + route_weight[:, route_index:route_index + 1] * cold[route_place[:, route_index]]
    for hot_index in range(HOT):
        chosen = hot_list[hot_index]
        weight = jnp.sum(jnp.where(expert_ids == chosen, gates, 0.0), axis=1)

        def hot_block(rows):
            return expert_apply(rows, w_gate[chosen], w_up[chosen], w_down[chosen])

        hot_out = lax.map(hot_block, tokens.reshape(N_EXPERT, TOK_DEV, D)).reshape(TOKENS, D)
        combined = combined + weight[:, None] * hot_out
    return combined.astype(jnp.bfloat16)
```

```python
import functools

import jax
import jax.numpy as jnp
from jax import lax
from jax.experimental import pallas as pl
from jax.experimental.pallas import tpu as pltpu
from jax.sharding import PartitionSpec as P

VMEM_LIMIT = 60 * 1024 * 1024


def dot(a, b):
    return jnp.dot(a, b, preferred_element_type=jnp.float32)


def gate_up_kernel(first, at_ref, *refs):
    near_ref, far_ref, gate_ref, up_ref = refs[:4]
    out_ref = refs[-1]
    half, width = near_ref.shape[0], gate_ref.shape[2]
    for side, rows_ref in enumerate((near_ref, far_ref)):
        rows = slice(side * half, (side + 1) * half)
        for place, part_ref in enumerate((gate_ref, up_ref)):
            value = dot(rows_ref[...], part_ref[0])
            if not first:
                value = value + refs[4][0, place, rows]
            out_ref[0, place, rows] = value


def hidden_kernel(at_ref, near_ref, far_ref, gate_ref, up_ref, total_ref, weight_ref, out_ref):
    half, width = near_ref.shape[0], gate_ref.shape[2]
    for local_index in range(weight_ref.shape[1]):

        @pl.when(pl.program_id(0) == local_index)
        def _():
            for side, rows_ref in enumerate((near_ref, far_ref)):
                rows = slice(side * half, (side + 1) * half)
                gate_value = dot(rows_ref[...], gate_ref[0]) + total_ref[0, 0, rows]
                up_value = dot(rows_ref[...], up_ref[0]) + total_ref[0, 1, rows]
                value = gate_value / (1.0 + jnp.exp(-gate_value)) * up_value
                value = value * weight_ref[rows, local_index : local_index + 1]
                columns = slice(local_index * width, (local_index + 1) * width)
                out_ref[rows, columns] = value.astype(jnp.bfloat16)


def down_kernel(at_ref, hidden_ref, down_ref, keep_ref, send_ref):
    half = keep_ref.shape[0]
    send_ref[...] = dot(hidden_ref[half:], down_ref[...]).astype(jnp.bfloat16)
    keep_ref[...] = dot(hidden_ref[:half], down_ref[...])


def gate_up(at, near, far, w_gate, w_up, total):
    local_count, _, width = w_gate.shape
    half, depth = near.shape
    rows_spec = pl.BlockSpec((half, depth), lambda i, at: (0, 0))
    part_spec = pl.BlockSpec((1, depth, width), lambda i, at: (i, at[0], 0))
    total_spec = pl.BlockSpec((1, 2, 2 * half, width), lambda i, at: (i, 0, 0, 0))
    first = total is None
    flops = 2 * local_count * 2 * half * depth * 2 * width
    return pl.pallas_call(
        functools.partial(gate_up_kernel, first),
        out_shape=jax.ShapeDtypeStruct((local_count, 2, 2 * half, width), jnp.float32),
        grid_spec=pltpu.PrefetchScalarGridSpec(
            num_scalar_prefetch=1,
            grid=(local_count,),
            in_specs=[rows_spec, rows_spec, part_spec, part_spec] + [total_spec] * (not first),
            out_specs=total_spec,
        ),
        compiler_params=pltpu.CompilerParams(vmem_limit_bytes=VMEM_LIMIT),
        cost_estimate=pl.CostEstimate(flops=flops, bytes_accessed=8 << 20, transcendentals=0),
    )(at, near, far, w_gate, w_up, *([] if first else [total]))


def hidden(at, near, far, w_gate, w_up, total, weight):
    local_count, _, width = w_gate.shape
    half, depth = near.shape
    rows_spec = pl.BlockSpec((half, depth), lambda i, at: (0, 0))
    part_spec = pl.BlockSpec((1, depth, width), lambda i, at: (i, at[0], 0))
    total_spec = pl.BlockSpec((1, 2, 2 * half, width), lambda i, at: (i, 0, 0, 0))
    flops = 2 * local_count * 2 * half * depth * 2 * width
    return pl.pallas_call(
        hidden_kernel,
        out_shape=jax.ShapeDtypeStruct((2 * half, local_count * width), jnp.bfloat16),
        grid_spec=pltpu.PrefetchScalarGridSpec(
            num_scalar_prefetch=1,
            grid=(local_count,),
            in_specs=[
                rows_spec,
                rows_spec,
                part_spec,
                part_spec,
                total_spec,
                pl.BlockSpec(weight.shape, lambda i, at: (0, 0)),
            ],
            out_specs=pl.BlockSpec((2 * half, local_count * width), lambda i, at: (0, 0)),
        ),
        compiler_params=pltpu.CompilerParams(vmem_limit_bytes=VMEM_LIMIT),
        cost_estimate=pl.CostEstimate(flops=flops, bytes_accessed=8 << 20, transcendentals=0),
    )(at, near, far, w_gate, w_up, total, weight)


def down(at, value, w_down, depth):
    row_count, width = value.shape
    half = row_count // 2
    cuts = 2 if depth % 256 == 0 else 1
    block = depth // cuts
    return pl.pallas_call(
        down_kernel,
        out_shape=(
            jax.ShapeDtypeStruct((half, depth), jnp.float32),
            jax.ShapeDtypeStruct((half, depth), jnp.bfloat16),
        ),
        grid_spec=pltpu.PrefetchScalarGridSpec(
            num_scalar_prefetch=1,
            grid=(cuts,),
            in_specs=[
                pl.BlockSpec((row_count, width), lambda i, at: (0, 0)),
                pl.BlockSpec((width, block), lambda i, at: (0, at[0] * cuts + i)),
            ],
            out_specs=[pl.BlockSpec((half, block), lambda i, at: (0, i))] * 2,
        ),
        compiler_params=pltpu.CompilerParams(vmem_limit_bytes=VMEM_LIMIT),
        cost_estimate=pl.CostEstimate(
            flops=2 * row_count * width * depth, bytes_accessed=4 << 20, transcendentals=0
        ),
    )(at, value, w_down)


def route_weights(expert_ids, gates, hot_list, expert_count, capacity):
    row_count = expert_ids.shape[0]
    numbers = jnp.arange(expert_count, dtype=jnp.int32)
    match = expert_ids[:, :, None] == numbers[None, None, :]
    weight = jnp.sum(jnp.where(match, gates[:, :, None], 0.0), axis=1)
    member = jnp.any(match, axis=1)
    order = jnp.arange(row_count)
    earlier = (order[:, None] > order[None, :]).astype(jnp.bfloat16)
    slot = dot(earlier, member.astype(jnp.bfloat16))
    hot = jnp.any(numbers[:, None] == hot_list[None, :], axis=1)
    kept = jnp.logical_and(member, jnp.logical_or(hot[None, :], slot < capacity))
    return jnp.where(kept, weight, 0.0)


def body(tokens, expert_ids, gates, hot_list, w_gate, w_up, w_down):
    owner_count, seq_count = lax.axis_size("expert"), lax.axis_size("seq")
    chip_count = owner_count // 2
    local_count, feature_count, width = w_gate.shape
    expert_count = local_count * owner_count
    row_count, pick_count = expert_ids.shape
    depth = tokens.shape[1]
    capacity = 3 * row_count * pick_count // (4 * expert_count)
    me, seq = lax.axis_index("expert"), lax.axis_index("seq")

    def over_seq(value, shift):
        if shift == 0:
            return value
        return lax.ppermute(value, "seq", [(i, (i + shift) % seq_count) for i in range(seq_count)])

    def over_chips(value, shift):
        if shift % chip_count == 0:
            return value
        return lax.ppermute(
            value,
            "expert",
            [
                (2 * i + c, 2 * ((i + shift) % chip_count) + c)
                for i in range(chip_count)
                for c in range(2)
            ],
        )

    def over_core(value):
        return lax.ppermute(value, "expert", [(i, i ^ 1) for i in range(owner_count)])

    def gathered(value):
        near = jnp.concatenate([over_chips(value, shift) for shift in range(chip_count)], axis=0)
        return near, over_core(near)

    shifts = [s for k in range(seq_count) for s in {k, (-k) % seq_count} if k <= seq_count // 2]
    weights = route_weights(expert_ids, gates, hot_list, expert_count, capacity)
    pieces = [(shift, over_seq(tokens, shift)) for shift in shifts]
    near_weights, far_weights = gathered(weights.T[None])
    own_weights = lax.dynamic_slice_in_dim(
        jnp.concatenate([near_weights, far_weights], axis=0), me * local_count, local_count, axis=1
    )
    own_weights = jnp.transpose(own_weights, (0, 2, 1)).reshape(-1, local_count)

    total = None
    for number, (shift, piece) in enumerate(pieces):
        near, far = gathered(piece)
        at = ((seq - shift) % seq_count).astype(jnp.int32).reshape(1)
        if number < len(pieces) - 1:
            total = gate_up(at, near, far, w_gate, w_up, total)
        else:
            value = hidden(at, near, far, w_gate, w_up, total, own_weights)

    flat_down = w_down.reshape(local_count * width, feature_count)
    moved = None
    for shift in shifts[::-1]:
        at = ((seq + shift) % seq_count).astype(jnp.int32).reshape(1)
        keep, send = down(at, value, flat_down, depth)
        pair = (keep + over_core(send).astype(jnp.float32)).reshape(chip_count, row_count, depth)
        row = pair[0]
        for chip in range(1, chip_count):
            row = row + over_chips(pair[chip].astype(jnp.bfloat16), -chip).astype(jnp.float32)
        term = row if shift == 0 else over_seq(row.astype(jnp.bfloat16), shift).astype(jnp.float32)
        moved = term if moved is None else moved + term
    return moved.astype(jnp.bfloat16)


def solution(mesh):
    placed = (
        P(("parts", "expert"), "seq"),
        P(("parts", "expert"), None),
        P(("parts", "expert"), None),
        P("parts"),
        P("expert", None, "seq"),
        P("expert", None, "seq"),
        P("expert", "seq", None),
    )
    return jax.shard_map(
        body, mesh=mesh, in_specs=placed, out_specs=P(("parts", "expert"), "seq"), check_vma=False
    )
```

```python
import functools

import jax
import jax.numpy as jnp
from jax import lax
from jax.experimental import pallas as pl
from jax.experimental.pallas import tpu as pltpu
from jax.sharding import PartitionSpec as P

VMEM_LIMIT = 16 * 1024 * 1024
COST = 8000000000
VMEM = pl.BlockSpec(memory_space=pltpu.VMEM)
HBM = pl.BlockSpec(memory_space=pltpu.HBM)
SMEM = pl.BlockSpec(memory_space=pltpu.SMEM)


def dot(a, b):
    return jnp.dot(a, b, preferred_element_type=jnp.float32)


def call(kernel, out_shape, in_specs, cost=COST, **more):
    many = isinstance(out_shape, (tuple, list))
    return pl.pallas_call(
        kernel,
        out_shape=out_shape,
        in_specs=in_specs,
        out_specs=[VMEM] * len(out_shape) if many else VMEM,
        compiler_params=pltpu.CompilerParams(vmem_limit_bytes=VMEM_LIMIT),
        cost_estimate=pl.CostEstimate(flops=cost, bytes_accessed=cost, transcendentals=0),
        **more,
    )


def in_hbm(value):
    return pltpu.with_memory_space_constraint(value, pltpu.HBM)


def in_vmem(value):
    return pltpu.with_memory_space_constraint(value, pltpu.VMEM)


def load_parts(sources, part_refs, sems, block):
    local_count, _, width = sources[0].shape
    depth = part_refs[0].shape[1]
    rows = pl.ds(pl.multiple_of(block * depth, depth), depth)
    loads = []
    for index in range(local_count):
        copies = []
        for side, source in enumerate(sources):
            if len(part_refs) == 1:
                target = part_refs[0].at[index, :, side * width : (side + 1) * width]
            else:
                target = part_refs[side].at[index]
            copies.append(
                pltpu.make_async_copy(source.at[index, rows], target, sems.at[2 * index + side])
            )
        loads.append(copies)
    return loads


def load_down(source, part_ref, sems, block):
    depth = part_ref.shape[2]
    columns = pl.ds(pl.multiple_of(block * depth, depth), depth)
    return [
        pltpu.make_async_copy(source.at[index, :, columns], part_ref.at[index], sems.at[index])
        for index in range(source.shape[0])
    ]


def start(copies):
    for copy in copies:
        copy.start()


def wait(copies):
    for copy in copies:
        copy.wait()


def products(rows, part_refs, index):
    parts = [dot(rows, part_ref[index]) for part_ref in part_refs]
    return parts[0] if len(parts) == 1 else jnp.concatenate(parts, axis=1)


def gate_up_kernel(first, at_ref, near_ref, far_ref, gate_ref, up_ref, *refs):
    total_ref, refs = (None, refs) if first else (refs[0], refs[1:])
    out_ref, part_refs, sems = refs[0], refs[1:-1], refs[-1]
    loads = load_parts([gate_ref, up_ref], part_refs, sems, at_ref[0])
    for copies in loads:
        start(copies)
    rows = jnp.concatenate([near_ref[...], far_ref[...]], axis=0)
    for index, copies in enumerate(loads):
        wait(copies)
        value = products(rows, part_refs, index)
        out_ref[index] = value if first else value + total_ref[index]


def down_product(value, part_ref, keep_ref, send_ref):
    half, width = keep_ref.shape[0], part_ref.shape[1]
    if width % 128 == 0:
        parts = [part_ref[index] for index in range(part_ref.shape[0])]
        result = dot(value, jnp.concatenate(parts, axis=0))
    else:
        result = 0.0
        for index in range(part_ref.shape[0]):
            result += dot(value[:, index * width : (index + 1) * width], part_ref[index])
    send_ref[...] = result[half:].astype(jnp.bfloat16)
    keep_ref[...] = result[:half]


def last_load_kernel(at_ref, gate_ref, up_ref, down_ref, *refs):
    part_refs, (down_part, sems, down_sems) = refs[:-3], refs[-3:]
    loads = load_parts([gate_ref, up_ref], part_refs, sems, at_ref[0])
    loads.append(load_down(down_ref, down_part, down_sems, at_ref[1]))
    for copies in loads:
        start(copies)
    for copies in loads:
        wait(copies)


def hidden_kernel(near_ref, far_ref, total_ref, weight_ref, *refs):
    part_refs, (down_part, out_ref, keep_ref, send_ref) = refs[:-4], refs[-4:]
    width = total_ref.shape[2] // 2
    rows = jnp.concatenate([near_ref[...], far_ref[...]], axis=0)
    for index in range(total_ref.shape[0]):
        value = products(rows, part_refs, index) + total_ref[index]
        gate_value, up_value = value[:, :width], value[:, width:]
        value = gate_value / (1.0 + jnp.exp(-gate_value)) * up_value
        value = value * weight_ref[:, index : index + 1]
        out_ref[:, index * width : (index + 1) * width] = value.astype(jnp.bfloat16)
    down_product(out_ref[...], down_part, keep_ref, send_ref)


def down_kernel(at_ref, hidden_ref, down_ref, keep_ref, send_ref, part_ref, sems):
    copies = load_down(down_ref, part_ref, sems, at_ref[0])
    start(copies)
    wait(copies)
    down_product(hidden_ref[...], part_ref, keep_ref, send_ref)


def part_scratch(w_gate, depth):
    local_count, _, width = w_gate.shape
    aligned = width % 128 == 0
    shape = (local_count, depth, 2 * width if aligned else width)
    return [pltpu.VMEM(shape, w_gate.dtype)] * (1 if aligned else 2)


def down_scratch(w_down, depth):
    return pltpu.VMEM((w_down.shape[0], w_down.shape[1], depth), w_down.dtype)


def down_shapes(half, depth):
    return [
        jax.ShapeDtypeStruct((half, depth), jnp.float32),
        jax.ShapeDtypeStruct((half, depth), jnp.bfloat16),
    ]


def gate_up(at, near, far, w_gate, w_up, total):
    local_count, _, width = w_gate.shape
    half, depth = near.shape
    totals = [] if total is None else [total]
    return call(
        functools.partial(gate_up_kernel, total is None),
        jax.ShapeDtypeStruct((local_count, 2 * half, 2 * width), jnp.float32),
        [SMEM, VMEM, VMEM, HBM, HBM] + [VMEM] * len(totals),
        scratch_shapes=part_scratch(w_gate, depth) + [pltpu.SemaphoreType.DMA((2 * local_count,))],
    )(at, near, far, in_hbm(w_gate), in_hbm(w_up), *totals)


def last_load(at, w_gate, w_up, w_down, depth):
    local_count = w_gate.shape[0]
    return call(
        last_load_kernel,
        part_scratch(w_gate, depth) + [down_scratch(w_down, depth)],
        [SMEM, HBM, HBM, HBM],
        scratch_shapes=[
            pltpu.SemaphoreType.DMA((2 * local_count,)),
            pltpu.SemaphoreType.DMA((local_count,)),
        ],
    )(at, in_hbm(w_gate), in_hbm(w_up), in_hbm(w_down))


def hidden(near, far, total, weight, parts):
    local_count, row_count, width = total.shape
    half, depth = near.shape
    return call(
        hidden_kernel,
        [jax.ShapeDtypeStruct((row_count, local_count * width // 2), jnp.bfloat16)]
        + down_shapes(half, depth),
        [VMEM] * (4 + len(parts)),
    )(near, far, total, weight, *map(in_vmem, parts))


def down(at, value, w_down, depth):
    return call(
        down_kernel,
        down_shapes(value.shape[0] // 2, depth),
        [SMEM, VMEM, HBM],
        scratch_shapes=[
            down_scratch(w_down, depth),
            pltpu.SemaphoreType.DMA((w_down.shape[0],)),
        ],
    )(at, value, in_hbm(w_down))


def route_weights(expert_ids, gates, hot_list, expert_count, capacity):
    row_count = expert_ids.shape[0]
    numbers = jnp.arange(expert_count, dtype=jnp.int32)
    match = expert_ids[:, :, None] == numbers[None, None, :]
    weight = jnp.sum(jnp.where(match, gates[:, :, None], 0.0), axis=1)
    member = jnp.any(match, axis=1)
    order = jnp.arange(row_count)
    earlier = (order[:, None] > order[None, :]).astype(jnp.bfloat16)
    slot = dot(earlier, member.astype(jnp.bfloat16))
    hot = jnp.any(numbers[:, None] == hot_list[None, :], axis=1)
    kept = jnp.logical_and(member, jnp.logical_or(hot[None, :], slot < capacity))
    return jnp.where(kept, weight, 0.0)


def body(tokens, expert_ids, gates, hot_list, w_gate, w_up, w_down):
    owner_count, seq_count = lax.axis_size("expert"), lax.axis_size("seq")
    chip_count = owner_count // 2
    local_count, feature_count, width = w_gate.shape
    expert_count = local_count * owner_count
    row_count, pick_count = expert_ids.shape
    depth = tokens.shape[1]
    capacity = 3 * row_count * pick_count // (4 * expert_count)
    me, seq = lax.axis_index("expert"), lax.axis_index("seq")

    def over_seq(value, flip):
        return lax.ppermute(value, "seq", [(i, i ^ flip) for i in range(seq_count)])

    def over_chips(value, shift):
        if shift % chip_count == 0:
            return value
        return lax.ppermute(
            value,
            "expert",
            [
                (2 * i + c, 2 * ((i + shift) % chip_count) + c)
                for i in range(chip_count)
                for c in range(2)
            ],
        )

    def over_core(value):
        return lax.ppermute(value, "expert", [(i, i ^ 1) for i in range(owner_count)])

    def gathered(value):
        near = jnp.concatenate([over_chips(value, shift) for shift in range(chip_count)], axis=0)
        return near, over_core(near)

    weights = route_weights(expert_ids, gates, hot_list, expert_count, capacity)
    near_weights, far_weights = gathered(weights.T[None])
    own_weights = lax.dynamic_slice_in_dim(
        jnp.concatenate([near_weights, far_weights], axis=0), me * local_count, local_count, axis=1
    )
    own_weights = jnp.transpose(own_weights, (0, 2, 1)).reshape(-1, local_count)

    after = lax.optimization_barrier

    def places(flip):
        return (seq ^ flip).astype(jnp.int32).reshape(1)

    def both_chips(piece):
        return jnp.concatenate([over_chips(piece, c) for c in range(chip_count)], axis=0)

    gates = {'q1': ['p2'], 'm1': ['weights'], 'm2': ['t0'], 'm3': ['t2'], 'a0': ['t2']}
    last = seq_count - 1
    have = {"p0": tokens, "weights": own_weights, "w": weights}

    def both_chips(piece):
        return jnp.concatenate([over_chips(piece, c) for c in range(chip_count)], axis=0)

    def get(name):
        if name in have:
            return have[name]
        kind, flip = name[0], int(name[1:])
        if kind == "p":
            value = over_seq(get("p%d" % (flip & (flip - 1))), flip & -flip)
        elif kind == "q":
            value = get("p%d" % flip)
        elif kind == "n":
            value = both_chips(get("q%d" % flip))
        elif kind == "m":
            value = get("n%d" % flip)
        elif kind == "a":
            value = jnp.concatenate([places(last), places(last)])
        elif kind == "l":
            value = last_load(get("a0"), w_gate, w_up, w_down, depth)
        elif kind == "c":
            value = over_core(get("m%d" % flip))
        else:
            pair = get("m%d" % flip), get("c%d" % flip)
            before = get("t%d" % (flip - 1)) if flip else None
            if flip < last:
                value = gate_up(places(flip), *pair, w_gate, w_up, before)
            else:
                value, *have["first"] = hidden(*pair, before, get("weights"), get("l0"))
        for other in gates.get(name, ()):
            value, have[other] = after((value, get(other)))
        have[name] = value
        return value

    value = get("t%d" % last)
    pairs = {}
    for number, flip in enumerate(range(seq_count)[::-1]):
        if number >= 2:
            value, pairs[flip + 2] = after((value, pairs[flip + 2]))
        keep, send = have["first"] if flip == last else down(places(flip), value, w_down, depth)
        pairs[flip] = keep + over_core(send).astype(jnp.float32)
    rows = {}
    for flip in range(seq_count)[::-1]:
        pair = pairs[flip].reshape(chip_count, row_count, depth)
        row = pair[0]
        for chip in range(1, chip_count):
            row = row + over_chips(pair[chip].astype(jnp.bfloat16), -chip).astype(jnp.float32)
        rows[flip] = row
    for flip in range(1, seq_count)[::-1]:
        moved = over_seq(rows[flip].astype(jnp.bfloat16), flip & -flip).astype(jnp.float32)
        rows[flip & (flip - 1)] = rows[flip & (flip - 1)] + moved
    moved = rows[0]
    return moved.astype(jnp.bfloat16)


def solution(mesh):
    placed = (
        P(("parts", "expert"), "seq"),
        P(("parts", "expert"), None),
        P(("parts", "expert"), None),
        P("parts"),
        P("expert", None, "seq"),
        P("expert", None, "seq"),
        P("expert", "seq", None),
    )
    return jax.shard_map(
        body, mesh=mesh, in_specs=placed, out_specs=P(("parts", "expert"), "seq"), check_vma=False
    )
```

```python
import functools

import jax
import jax.numpy as jnp
from jax import lax
from jax.experimental import pallas as pl
from jax.experimental.pallas import tpu as pltpu
from jax.sharding import PartitionSpec as P

VMEM_LIMIT = 20 * 1024 * 1024
COST = 8000000000
VMEM = pl.BlockSpec(memory_space=pltpu.VMEM)
HBM = pl.BlockSpec(memory_space=pltpu.HBM)
SMEM = pl.BlockSpec(memory_space=pltpu.SMEM)


def dot(a, b):
    return jnp.dot(a, b, preferred_element_type=jnp.float32)


def call(kernel, out_shape, in_specs, cost=COST, **more):
    many = isinstance(out_shape, (tuple, list))
    return pl.pallas_call(
        kernel,
        out_shape=out_shape,
        in_specs=in_specs,
        out_specs=[VMEM] * len(out_shape) if many else VMEM,
        compiler_params=pltpu.CompilerParams(vmem_limit_bytes=VMEM_LIMIT),
        cost_estimate=pl.CostEstimate(flops=cost, bytes_accessed=cost, transcendentals=0),
        **more,
    )


def in_hbm(value):
    return pltpu.with_memory_space_constraint(value, pltpu.HBM)


def in_vmem(value):
    return pltpu.with_memory_space_constraint(value, pltpu.VMEM)


def load_parts(sources, part_refs, sems, block):
    local_count, _, width = sources[0].shape
    depth = part_refs[0].shape[1]
    rows = pl.ds(pl.multiple_of(block * depth, depth), depth)
    loads = []
    for index in range(local_count):
        copies = []
        for side, source in enumerate(sources):
            if len(part_refs) == 1:
                target = part_refs[0].at[index, :, side * width : (side + 1) * width]
            else:
                target = part_refs[side].at[index]
            copies.append(
                pltpu.make_async_copy(source.at[index, rows], target, sems.at[2 * index + side])
            )
        loads.append(copies)
    return loads


def load_down(source, part_ref, sems, block):
    depth = part_ref.shape[2]
    columns = pl.ds(pl.multiple_of(block * depth, depth), depth)
    return [
        pltpu.make_async_copy(source.at[index, :, columns], part_ref.at[index], sems.at[index])
        for index in range(source.shape[0])
    ]


def start(copies):
    for copy in copies:
        copy.start()


def wait(copies):
    for copy in copies:
        copy.wait()


def products(rows, part_refs, index):
    parts = [dot(rows, part_ref[index]) for part_ref in part_refs]
    return parts[0] if len(parts) == 1 else jnp.concatenate(parts, axis=1)


def gate_up_kernel(first, loads_down, at_ref, near_ref, far_ref, gate_ref, up_ref, *refs):
    refs = list(refs)
    per = 1 if gate_ref.shape[2] % 128 == 0 else 2
    down_ref = refs.pop(0) if loads_down else None
    total_ref = None if first else refs.pop(0)
    part_refs = None if first else [refs.pop(0) for _ in range(per)]
    out_ref = refs.pop(0)
    next_refs = [refs.pop(0) for _ in range(per)]
    down_part = refs.pop(0) if loads_down else None
    own_loads = []
    if first:
        part_refs = [refs.pop(0) for _ in range(per)]
        own_loads = load_parts([gate_ref, up_ref], part_refs, refs.pop(0), at_ref[0])
    next_loads = load_parts([gate_ref, up_ref], next_refs, refs.pop(0), at_ref[1])
    if loads_down:
        next_loads.append(load_down(down_ref, down_part, refs.pop(0), at_ref[1]))
    for copies in own_loads + next_loads:
        start(copies)
    rows = jnp.concatenate([near_ref[...], far_ref[...]], axis=0)
    for index in range(out_ref.shape[0]):
        if first:
            wait(own_loads[index])
        value = products(rows, part_refs, index)
        out_ref[index] = value if first else value + total_ref[index]
    for copies in next_loads:
        wait(copies)


def down_product(value, part_ref, keep_ref, send_ref):
    half, width = keep_ref.shape[0], part_ref.shape[1]
    if width % 128 == 0:
        parts = [part_ref[index] for index in range(part_ref.shape[0])]
        result = dot(value, jnp.concatenate(parts, axis=0))
    else:
        result = 0.0
        for index in range(part_ref.shape[0]):
            result += dot(value[:, index * width : (index + 1) * width], part_ref[index])
    send_ref[...] = result[half:].astype(jnp.bfloat16)
    keep_ref[...] = result[:half]


def hidden_kernel(near_ref, far_ref, total_ref, weight_ref, *refs):
    part_refs, (down_part, out_ref, keep_ref, send_ref) = refs[:-4], refs[-4:]
    width = total_ref.shape[2] // 2
    rows = jnp.concatenate([near_ref[...], far_ref[...]], axis=0)
    for index in range(total_ref.shape[0]):
        value = products(rows, part_refs, index) + total_ref[index]
        gate_value, up_value = value[:, :width], value[:, width:]
        value = gate_value / (1.0 + jnp.exp(-gate_value)) * up_value
        value = value * weight_ref[:, index : index + 1]
        out_ref[:, index * width : (index + 1) * width] = value.astype(jnp.bfloat16)
    down_product(out_ref[...], down_part, keep_ref, send_ref)


def down_kernel(at_ref, hidden_ref, down_ref, keep_ref, send_ref, part_ref, sems):
    copies = load_down(down_ref, part_ref, sems, at_ref[0])
    start(copies)
    wait(copies)
    down_product(hidden_ref[...], part_ref, keep_ref, send_ref)


def part_scratch(w_gate, depth):
    local_count, _, width = w_gate.shape
    aligned = width % 128 == 0
    shape = (local_count, depth, 2 * width if aligned else width)
    return [pltpu.VMEM(shape, w_gate.dtype)] * (1 if aligned else 2)


def down_scratch(w_down, depth):
    return pltpu.VMEM((w_down.shape[0], w_down.shape[1], depth), w_down.dtype)


def down_shapes(half, depth):
    return [
        jax.ShapeDtypeStruct((half, depth), jnp.float32),
        jax.ShapeDtypeStruct((half, depth), jnp.bfloat16),
    ]


def gate_up(at, near, far, w_gate, w_up, total, parts, w_down):
    local_count, _, width = w_gate.shape
    half, depth = near.shape
    first, loads_down = total is None, w_down is not None
    shapes = [jax.ShapeDtypeStruct((local_count, 2 * half, 2 * width), jnp.float32)]
    shapes += part_scratch(w_gate, depth)
    scratch = [pltpu.SemaphoreType.DMA((2 * local_count,))]
    if first:
        scratch = part_scratch(w_gate, depth) + scratch + scratch
    more, specs = [], []
    if loads_down:
        shapes.append(down_scratch(w_down, depth))
        scratch.append(pltpu.SemaphoreType.DMA((local_count,)))
        more.append(in_hbm(w_down))
        specs.append(HBM)
    if not first:
        more += [total, *map(in_vmem, parts)]
        specs += [VMEM] * (1 + len(parts))
    total, *parts = call(
        functools.partial(gate_up_kernel, first, loads_down),
        shapes,
        [SMEM, VMEM, VMEM, HBM, HBM] + specs,
        scratch_shapes=scratch,
    )(at, near, far, in_hbm(w_gate), in_hbm(w_up), *more)
    return total, parts


def hidden(near, far, total, weight, parts):
    local_count, row_count, width = total.shape
    half, depth = near.shape
    return call(
        hidden_kernel,
        [jax.ShapeDtypeStruct((row_count, local_count * width // 2), jnp.bfloat16)]
        + down_shapes(half, depth),
        [VMEM] * (4 + len(parts)),
    )(near, far, total, weight, *map(in_vmem, parts))


def down(at, value, w_down, depth):
    return call(
        down_kernel,
        down_shapes(value.shape[0] // 2, depth),
        [SMEM, VMEM, HBM],
        scratch_shapes=[
            down_scratch(w_down, depth),
            pltpu.SemaphoreType.DMA((w_down.shape[0],)),
        ],
    )(at, value, in_hbm(w_down))


def route_weights(expert_ids, gates, hot_list, expert_count, capacity):
    row_count = expert_ids.shape[0]
    numbers = jnp.arange(expert_count, dtype=jnp.int32)
    match = expert_ids[:, :, None] == numbers[None, None, :]
    weight = jnp.sum(jnp.where(match, gates[:, :, None], 0.0), axis=1)
    member = jnp.any(match, axis=1)
    order = jnp.arange(row_count)
    earlier = (order[:, None] > order[None, :]).astype(jnp.bfloat16)
    slot = dot(earlier, member.astype(jnp.bfloat16))
    hot = jnp.any(numbers[:, None] == hot_list[None, :], axis=1)
    kept = jnp.logical_and(member, jnp.logical_or(hot[None, :], slot < capacity))
    return jnp.where(kept, weight, 0.0)


def body(tokens, expert_ids, gates, hot_list, w_gate, w_up, w_down):
    owner_count, seq_count = lax.axis_size("expert"), lax.axis_size("seq")
    chip_count = owner_count // 2
    local_count, feature_count, width = w_gate.shape
    expert_count = local_count * owner_count
    row_count, pick_count = expert_ids.shape
    depth = tokens.shape[1]
    capacity = 3 * row_count * pick_count // (4 * expert_count)
    me, seq = lax.axis_index("expert"), lax.axis_index("seq")

    def over_seq(value, flip):
        return lax.ppermute(value, "seq", [(i, i ^ flip) for i in range(seq_count)])

    def over_chips(value, shift):
        if shift % chip_count == 0:
            return value
        return lax.ppermute(
            value,
            "expert",
            [
                (2 * i + c, 2 * ((i + shift) % chip_count) + c)
                for i in range(chip_count)
                for c in range(2)
            ],
        )

    def over_core(value):
        return lax.ppermute(value, "expert", [(i, i ^ 1) for i in range(owner_count)])

    def gathered(value):
        near = jnp.concatenate([over_chips(value, shift) for shift in range(chip_count)], axis=0)
        return near, over_core(near)

    weights = route_weights(expert_ids, gates, hot_list, expert_count, capacity)
    near_weights, far_weights = gathered(weights.T[None])
    own_weights = lax.dynamic_slice_in_dim(
        jnp.concatenate([near_weights, far_weights], axis=0), me * local_count, local_count, axis=1
    )
    own_weights = jnp.transpose(own_weights, (0, 2, 1)).reshape(-1, local_count)

    after = lax.optimization_barrier

    def places(flip):
        return (seq ^ flip).astype(jnp.int32).reshape(1)

    def both_chips(piece):
        return jnp.concatenate([over_chips(piece, c) for c in range(chip_count)], axis=0)

    gates = {'q1': ['p2'], 'm1': ['weights'], 'm2': ['t0']}
    last = seq_count - 1
    have = {"p0": tokens, "weights": own_weights, "w": weights}

    def both_chips(piece):
        return jnp.concatenate([over_chips(piece, c) for c in range(chip_count)], axis=0)

    def get(name):
        if name in have:
            return have[name]
        kind, flip = name[0], int(name[1:])
        if kind == "p":
            value = over_seq(get("r%d" % flip), flip & -flip)
        elif kind == "r":
            value = get("p%d" % (flip & (flip - 1)))
        elif kind == "q":
            value = get("p%d" % flip)
        elif kind == "n":
            value = both_chips(get("q%d" % flip))
        elif kind == "m":
            value = get("n%d" % flip)
        elif kind == "c":
            value = over_core(get("m%d" % flip))
        else:
            before = get("t%d" % (flip - 1)) if flip else None
            pair = get("m%d" % flip), get("c%d" % flip)
            parts = have.get("parts")
            if flip < last:
                at = jnp.concatenate([places(flip), places(flip + 1)])
                late = w_down if flip == last - 1 else None
                value, have["parts"] = gate_up(at, *pair, w_gate, w_up, before, parts, late)
            else:
                value, *have["first"] = hidden(*pair, before, get("weights"), parts)
        for other in gates.get(name, ()):
            value, have[other] = after((value, get(other)))
        have[name] = value
        return value

    value = get("t%d" % last)
    pairs = {}
    for number, flip in enumerate(range(seq_count)[::-1]):
        if number >= 2:
            value, pairs[flip + 2] = after((value, pairs[flip + 2]))
        keep, send = have["first"] if flip == last else down(places(flip), value, w_down, depth)
        pairs[flip] = keep + over_core(send).astype(jnp.float32)
    rows = {}
    for flip in range(seq_count)[::-1]:
        pair = pairs[flip].reshape(chip_count, row_count, depth)
        row = pair[0]
        for chip in range(1, chip_count):
            row = row + over_chips(pair[chip].astype(jnp.bfloat16), -chip).astype(jnp.float32)
        rows[flip] = row
    for flip in range(1, seq_count)[::-1]:
        moved = over_seq(rows[flip].astype(jnp.bfloat16), flip & -flip).astype(jnp.float32)
        rows[flip & (flip - 1)] = rows[flip & (flip - 1)] + moved
    moved = rows[0]
    return moved.astype(jnp.bfloat16)


def solution(mesh):
    placed = (
        P(("parts", "expert"), "seq"),
        P(("parts", "expert"), None),
        P(("parts", "expert"), None),
        P("parts"),
        P("expert", None, "seq"),
        P("expert", None, "seq"),
        P("expert", "seq", None),
    )
    return jax.shard_map(
        body, mesh=mesh, in_specs=placed, out_specs=P(("parts", "expert"), "seq"), check_vma=False
    )
```

```python
import functools

import jax
import jax.numpy as jnp
from jax import lax
from jax.experimental import pallas as pl
from jax.experimental.pallas import tpu as pltpu
from jax.sharding import PartitionSpec as P

CUTS = 2
VMEM_LIMIT = 20 * 1024 * 1024
COST = 8000000000
VMEM = pl.BlockSpec(memory_space=pltpu.VMEM)
HBM = pl.BlockSpec(memory_space=pltpu.HBM)
SMEM = pl.BlockSpec(memory_space=pltpu.SMEM)


def dot(a, b):
    return jnp.dot(a, b, preferred_element_type=jnp.float32)


def call(kernel, out_shape, in_specs, cost=COST, **more):
    many = isinstance(out_shape, (tuple, list))
    return pl.pallas_call(
        kernel,
        out_shape=out_shape,
        in_specs=in_specs,
        out_specs=[VMEM] * len(out_shape) if many else VMEM,
        compiler_params=pltpu.CompilerParams(vmem_limit_bytes=VMEM_LIMIT),
        cost_estimate=pl.CostEstimate(flops=cost, bytes_accessed=cost, transcendentals=0),
        **more,
    )


def in_hbm(value):
    return pltpu.with_memory_space_constraint(value, pltpu.HBM)


def in_vmem(value):
    return pltpu.with_memory_space_constraint(value, pltpu.VMEM)


def load_parts(sources, part_refs, sems, block):
    local_count, _, width = sources[0].shape
    depth = part_refs[0].shape[1]
    cut = depth // CUTS
    loads = []
    for index in range(local_count):
        copies = []
        for side, source in enumerate(sources):
            for k in range(CUTS):
                rows = pl.ds(pl.multiple_of(block * depth + k * cut, cut), cut)
                if len(part_refs) == 1:
                    columns = slice(side * width, (side + 1) * width)
                    target = part_refs[0].at[index, k * cut : (k + 1) * cut, columns]
                else:
                    target = part_refs[side].at[index, k * cut : (k + 1) * cut]
                sem = sems.at[(2 * index + side) * CUTS + k]
                copies.append(pltpu.make_async_copy(source.at[index, rows], target, sem))
        loads.append(copies)
    return loads


def load_down(source, part_ref, sems, block):
    depth = part_ref.shape[2]
    columns = pl.ds(pl.multiple_of(block * depth, depth), depth)
    return [
        pltpu.make_async_copy(source.at[index, :, columns], part_ref.at[index], sems.at[index])
        for index in range(source.shape[0])
    ]


def start(copies):
    for copy in copies:
        copy.start()


def wait(copies):
    for copy in copies:
        copy.wait()


def products(rows, part_refs, index):
    parts = [dot(rows, part_ref[index]) for part_ref in part_refs]
    return parts[0] if len(parts) == 1 else jnp.concatenate(parts, axis=1)


def gate_up_kernel(first, loads_down, at_ref, near_ref, far_ref, gate_ref, up_ref, *refs):
    refs = list(refs)
    per = 1 if gate_ref.shape[2] % 128 == 0 else 2
    down_ref = refs.pop(0) if loads_down else None
    total_ref = None if first else refs.pop(0)
    part_refs = None if first else [refs.pop(0) for _ in range(per)]
    out_ref = refs.pop(0)
    next_refs = [refs.pop(0) for _ in range(per)]
    down_part = refs.pop(0) if loads_down else None
    own_loads = []
    if first:
        part_refs = [refs.pop(0) for _ in range(per)]
        own_loads = load_parts([gate_ref, up_ref], part_refs, refs.pop(0), at_ref[0])
    next_loads = load_parts([gate_ref, up_ref], next_refs, refs.pop(0), at_ref[1])
    if loads_down:
        next_loads.append(load_down(down_ref, down_part, refs.pop(0), at_ref[1]))
    for copies in own_loads + next_loads:
        start(copies)
    rows = jnp.concatenate([near_ref[...], far_ref[...]], axis=0)
    for index in range(out_ref.shape[0]):
        if first:
            wait(own_loads[index])
        value = products(rows, part_refs, index)
        out_ref[index] = value if first else value + total_ref[index]
    for copies in next_loads:
        wait(copies)


def down_product(value, part_ref, keep_ref, send_ref):
    half, width = keep_ref.shape[0], part_ref.shape[1]
    if width % 128 == 0:
        parts = [part_ref[index] for index in range(part_ref.shape[0])]
        result = dot(value, jnp.concatenate(parts, axis=0))
    else:
        result = 0.0
        for index in range(part_ref.shape[0]):
            result += dot(value[:, index * width : (index + 1) * width], part_ref[index])
    send_ref[...] = result[half:].astype(jnp.bfloat16)
    keep_ref[...] = result[:half]


def hidden_kernel(near_ref, far_ref, total_ref, weight_ref, *refs):
    part_refs, (down_part, out_ref, keep_ref, send_ref) = refs[:-4], refs[-4:]
    width = total_ref.shape[2] // 2
    rows = jnp.concatenate([near_ref[...], far_ref[...]], axis=0)
    for index in range(total_ref.shape[0]):
        value = products(rows, part_refs, index) + total_ref[index]
        gate_value, up_value = value[:, :width], value[:, width:]
        value = gate_value / (1.0 + jnp.exp(-gate_value)) * up_value
        value = value * weight_ref[:, index : index + 1]
        out_ref[:, index * width : (index + 1) * width] = value.astype(jnp.bfloat16)
    down_product(out_ref[...], down_part, keep_ref, send_ref)


def down_kernel(at_ref, hidden_ref, down_ref, keep_ref, send_ref, part_ref, sems):
    copies = load_down(down_ref, part_ref, sems, at_ref[0])
    start(copies)
    wait(copies)
    down_product(hidden_ref[...], part_ref, keep_ref, send_ref)


def part_scratch(w_gate, depth):
    local_count, _, width = w_gate.shape
    aligned = width % 128 == 0
    shape = (local_count, depth, 2 * width if aligned else width)
    return [pltpu.VMEM(shape, w_gate.dtype)] * (1 if aligned else 2)


def down_scratch(w_down, depth):
    return pltpu.VMEM((w_down.shape[0], w_down.shape[1], depth), w_down.dtype)


def down_shapes(half, depth):
    return [
        jax.ShapeDtypeStruct((half, depth), jnp.float32),
        jax.ShapeDtypeStruct((half, depth), jnp.bfloat16),
    ]


def gate_up(at, near, far, w_gate, w_up, total, parts, w_down):
    local_count, _, width = w_gate.shape
    half, depth = near.shape
    first, loads_down = total is None, w_down is not None
    shapes = [jax.ShapeDtypeStruct((local_count, 2 * half, 2 * width), jnp.float32)]
    shapes += part_scratch(w_gate, depth)
    scratch = [pltpu.SemaphoreType.DMA((2 * local_count * CUTS,))]
    if first:
        scratch = part_scratch(w_gate, depth) + scratch + scratch
    more, specs = [], []
    if loads_down:
        shapes.append(down_scratch(w_down, depth))
        scratch.append(pltpu.SemaphoreType.DMA((local_count,)))
        more.append(in_hbm(w_down))
        specs.append(HBM)
    if not first:
        more += [total, *map(in_vmem, parts)]
        specs += [VMEM] * (1 + len(parts))
    total, *parts = call(
        functools.partial(gate_up_kernel, first, loads_down),
        shapes,
        [SMEM, VMEM, VMEM, HBM, HBM] + specs,
        scratch_shapes=scratch,
    )(at, near, far, in_hbm(w_gate), in_hbm(w_up), *more)
    return total, parts


def hidden(near, far, total, weight, parts):
    local_count, row_count, width = total.shape
    half, depth = near.shape
    return call(
        hidden_kernel,
        [jax.ShapeDtypeStruct((row_count, local_count * width // 2), jnp.bfloat16)]
        + down_shapes(half, depth),
        [VMEM] * (4 + len(parts)),
    )(near, far, total, weight, *map(in_vmem, parts))


def down(at, value, w_down, depth):
    return call(
        down_kernel,
        down_shapes(value.shape[0] // 2, depth),
        [SMEM, VMEM, HBM],
        scratch_shapes=[
            down_scratch(w_down, depth),
            pltpu.SemaphoreType.DMA((w_down.shape[0],)),
        ],
    )(at, value, in_hbm(w_down))


def route_weights(expert_ids, gates, hot_list, expert_count, capacity):
    row_count = expert_ids.shape[0]
    numbers = jnp.arange(expert_count, dtype=jnp.int32)
    match = expert_ids[:, :, None] == numbers[None, None, :]
    weight = jnp.sum(jnp.where(match, gates[:, :, None], 0.0), axis=1)
    member = jnp.any(match, axis=1)
    order = jnp.arange(row_count)
    earlier = (order[:, None] > order[None, :]).astype(jnp.bfloat16)
    slot = dot(earlier, member.astype(jnp.bfloat16))
    hot = jnp.any(numbers[:, None] == hot_list[None, :], axis=1)
    kept = jnp.logical_and(member, jnp.logical_or(hot[None, :], slot < capacity))
    return jnp.where(kept, weight, 0.0)


def body(tokens, expert_ids, gates, hot_list, w_gate, w_up, w_down):
    owner_count, seq_count = lax.axis_size("expert"), lax.axis_size("seq")
    chip_count = owner_count // 2
    local_count, feature_count, width = w_gate.shape
    expert_count = local_count * owner_count
    row_count, pick_count = expert_ids.shape
    depth = tokens.shape[1]
    capacity = 3 * row_count * pick_count // (4 * expert_count)
    me, seq = lax.axis_index("expert"), lax.axis_index("seq")

    def over_seq(value, flip):
        return lax.ppermute(value, "seq", [(i, i ^ flip) for i in range(seq_count)])

    def over_chips(value, shift):
        if shift % chip_count == 0:
            return value
        return lax.ppermute(
            value,
            "expert",
            [
                (2 * i + c, 2 * ((i + shift) % chip_count) + c)
                for i in range(chip_count)
                for c in range(2)
            ],
        )

    def over_core(value):
        return lax.ppermute(value, "expert", [(i, i ^ 1) for i in range(owner_count)])

    def gathered(value):
        near = jnp.concatenate([over_chips(value, shift) for shift in range(chip_count)], axis=0)
        return near, over_core(near)

    weights = route_weights(expert_ids, gates, hot_list, expert_count, capacity)
    near_weights, far_weights = gathered(weights.T[None])
    own_weights = lax.dynamic_slice_in_dim(
        jnp.concatenate([near_weights, far_weights], axis=0), me * local_count, local_count, axis=1
    )
    own_weights = jnp.transpose(own_weights, (0, 2, 1)).reshape(-1, local_count)

    after = lax.optimization_barrier

    def places(flip):
        return (seq ^ flip).astype(jnp.int32).reshape(1)

    def both_chips(piece):
        return jnp.concatenate([over_chips(piece, c) for c in range(chip_count)], axis=0)

    gates = {'q1': ['p2'], 'm1': ['weights'], 'm2': ['t0']}
    last = seq_count - 1
    have = {"p0": tokens, "weights": own_weights, "w": weights}

    def both_chips(piece):
        return jnp.concatenate([over_chips(piece, c) for c in range(chip_count)], axis=0)

    def get(name):
        if name in have:
            return have[name]
        kind, flip = name[0], int(name[1:])
        if kind == "p":
            value = over_seq(get("r%d" % flip), flip & -flip)
        elif kind == "r":
            value = get("p%d" % (flip & (flip - 1)))
        elif kind == "q":
            value = get("p%d" % flip)
        elif kind == "n":
            value = both_chips(get("q%d" % flip))
        elif kind == "m":
            value = get("n%d" % flip)
        elif kind == "c":
            value = over_core(get("m%d" % flip))
        else:
            before = get("t%d" % (flip - 1)) if flip else None
            pair = get("m%d" % flip), get("c%d" % flip)
            parts = have.get("parts")
            if flip < last:
                at = jnp.concatenate([places(flip), places(flip + 1)])
                late = w_down if flip == last - 1 else None
                value, have["parts"] = gate_up(at, *pair, w_gate, w_up, before, parts, late)
            else:
                value, *have["first"] = hidden(*pair, before, get("weights"), parts)
        for other in gates.get(name, ()):
            value, have[other] = after((value, get(other)))
        have[name] = value
        return value

    value = get("t%d" % last)
    pairs = {}
    for number, flip in enumerate(range(seq_count)[::-1]):
        if number >= 2:
            value, pairs[flip + 2] = after((value, pairs[flip + 2]))
        keep, send = have["first"] if flip == last else down(places(flip), value, w_down, depth)
        pairs[flip] = keep + over_core(send).astype(jnp.float32)
    rows = {}
    for flip in range(seq_count)[::-1]:
        pair = pairs[flip].reshape(chip_count, row_count, depth)
        row = pair[0]
        for chip in range(1, chip_count):
            row = row + over_chips(pair[chip].astype(jnp.bfloat16), -chip).astype(jnp.float32)
        rows[flip] = row
    for flip in range(1, seq_count)[::-1]:
        moved = over_seq(rows[flip].astype(jnp.bfloat16), flip & -flip).astype(jnp.float32)
        rows[flip & (flip - 1)] = rows[flip & (flip - 1)] + moved
    moved = rows[0]
    return moved.astype(jnp.bfloat16)


def solution(mesh):
    placed = (
        P(("parts", "expert"), "seq"),
        P(("parts", "expert"), None),
        P(("parts", "expert"), None),
        P("parts"),
        P("expert", None, "seq"),
        P("expert", None, "seq"),
        P("expert", "seq", None),
    )
    return jax.shard_map(
        body, mesh=mesh, in_specs=placed, out_specs=P(("parts", "expert"), "seq"), check_vma=False
    )
```
